32 devices in a mesh: pipe: 2 (over core), tensor: 4 (over z), dp: 4 (over y, x).
Axes of the slice: x: 2, y: 2, z: 4, core: 2. Of those that a mesh axis runs over, the one named last changes fastest.
Arguments:
- section_input: bfloat16 [8, 256, 2048], P('dp', 'tensor'), may hold values from -6 to 6
- cotangent: bfloat16 [8, 256, 2048], P('dp', 'tensor'), may hold values from -6 to 6
- w_query: bfloat16 [2, 2048, 2048], P('pipe', 'dp', 'tensor'), may hold values from -0.125 to 0.125
- keyvalue_weight: bfloat16 [2, 2, 2048, 1024], P('pipe', None, 'dp', 'tensor'), may hold values from -0.125 to 0.125
- w_out: bfloat16 [2, 2048, 2048], P('pipe', 'tensor', 'dp'), may hold values from -0.5 to 0.5
- w_gateup: bfloat16 [2, 2, 2048, 6144], P('pipe', None, 'dp', 'tensor'), may hold values from -0.125 to 0.125
- w_down: bfloat16 [2, 6144, 2048], P('pipe', 'tensor', 'dp'), may hold values from -0.078125 to 0.078125
- norm_gains: bfloat16 [2, 2, 2048], P('pipe', None, 'dp'), may hold values from 0.5 to 1.5
- head_gains: bfloat16 [2, 2, 128], P('pipe', None, 'dp'), may hold values from 0.5 to 1.5
Outputs:
- section_out: bfloat16 [2, 8, 256, 2048], P('pipe', 'dp', 'tensor')
- input_grads: bfloat16 [2, 8, 256, 2048], P('pipe', 'dp', 'tensor')
- grad_query: float32 [2, 2048, 2048], P('pipe', 'dp', 'tensor')
- grad_keyval: float32 [2, 2, 2048, 1024], P('pipe', None, 'dp', 'tensor')
- grad_out: float32 [2, 2048, 2048], P('pipe', 'tensor', 'dp')
- grad_gateup: float32 [2, 2, 2048, 6144], P('pipe', None, 'dp', 'tensor')
- grad_down: float32 [2, 6144, 2048], P('pipe', 'tensor', 'dp')
- grad_norm_gains: float32 [2, 2, 2048], P('pipe', None, 'dp')
- grad_head_gains: float32 [2, 2, 128], P('pipe', None, 'dp')
The draws below stay inside these ranges and needn't reach their ends.
All inputs are finite; a program needn't handle non-finite values.
Results may differ from the reference program's by a relative error of at most 0.035.
Values may be sent and summed in bfloat16 or wider, within the bound.
A program may use at most 192 MiB of HBM per device.

```python
import jax
import jax.numpy as jnp
from jax import lax

MODEL_DIM = 2048
QUERY_COUNT = 16
KEYVALUE_HEADS = 8
HEAD_DIM = 128
FF = 6144
SEQ = 256
MICRO = 2
SEQS = 8


def level_of(stream_key, extent, pieces, smallest, top_value):
    loudness = 1.0
    for position, blocks in pieces:
        draws = jax.random.uniform(jax.random.fold_in(jax.random.fold_in(stream_key, 6), position), (blocks,), jnp.float32, smallest / len(pieces), top_value / len(pieces))
        loudness = loudness * jnp.repeat(jnp.exp(draws), extent[position] // blocks).reshape((-1,) + (1,) * (len(extent) - 1 - position))
    return loudness


def centred(stream_key, dims, width, bound, shards=(), held_as=jnp.bfloat16):
    values = width * jax.random.normal(stream_key, dims, jnp.float32)
    if shards:
        values = values * level_of(stream_key, dims, shards, -0.22, 0.18)
    return jnp.clip(values, -bound, bound).astype(held_as)


def setup_inputs(seed: int = 0) -> dict:
    splits = jax.random.split(jax.random.key(seed), 10)
    return {
        "section_input": centred(splits[0], (SEQS, SEQ, MODEL_DIM), 1.0, 6.0, ((0, 4), (1, 4))),
        "cotangent": centred(splits[1], (SEQS, SEQ, MODEL_DIM), 1.0, 6.0, ((0, 4), (1, 4))),
        "w_query": centred(splits[2], (2, MODEL_DIM, QUERY_COUNT * HEAD_DIM), MODEL_DIM ** -0.5, 0.125, ((0, 2), (1, 4), (2, 4))),
        "keyvalue_weight": centred(splits[3], (2, 2, MODEL_DIM, KEYVALUE_HEADS * HEAD_DIM), MODEL_DIM ** -0.5, 0.125, ((0, 2), (2, 4), (3, 4))),
        "w_out": centred(splits[4], (2, QUERY_COUNT * HEAD_DIM, MODEL_DIM), (QUERY_COUNT * HEAD_DIM * 16 // SEQ) ** -0.5, 0.5, ((0, 2), (1, 4), (2, 4))),
        "w_gateup": centred(splits[5], (2, 2, MODEL_DIM, FF), MODEL_DIM ** -0.5, 0.125, ((0, 2), (2, 4), (3, 4))),
        "w_down": centred(splits[6], (2, FF, MODEL_DIM), FF ** -0.5, 0.078125, ((0, 2), (1, 4), (2, 4))),
        "norm_gains": jnp.clip(1.0 + 0.1 * jax.random.normal(splits[7], (2, 2, MODEL_DIM), jnp.float32), 0.5, 1.5).astype(jnp.bfloat16),
        "head_gains": jnp.clip(1.0 + 0.1 * jax.random.normal(splits[8], (2, 2, HEAD_DIM), jnp.float32), 0.5, 1.5).astype(jnp.bfloat16),
    }


@jax.custom_vjp
def lowered_input(v):
    return lax.optimization_barrier(v.astype(jnp.bfloat16)).astype(jnp.float32)

@jax.custom_vjp
def lowered_gradient(v):
    return v

def low_keep(v):
    return (lowered_input(v), None)

def low_pass(kept, grad):
    return (grad,)

def back_keep(v):
    return (v, None)

def back_low(kept, grad):
    return (lowered_input(grad),)
lowered_input.defvjp(low_keep, low_pass)
lowered_gradient.defvjp(back_keep, back_low)
epsilon = 1e-06
theta_base = 1000000.0
highest = lax.Precision.HIGHEST

def rms_apply(values, gain_vec):
    inverse = lax.rsqrt(lax.optimization_barrier(jnp.mean(values * values, axis=-1, keepdims=True)) + epsilon)
    return values * inverse * gain_vec

def rope_tables(sequence_length, head_width):
    half_width = head_width // 2
    frequency = theta_base ** (-2.0 * jnp.arange(half_width, dtype=jnp.float32) / head_width)
    angles = jnp.arange(sequence_length, dtype=jnp.float32)[:, None] * frequency[None, :]
    angles = jnp.concatenate([angles, angles], axis=-1)
    return (jnp.cos(angles), jnp.sin(angles))

def rotate_pairs(values, cos_table, sine_table):
    half_width = values.shape[-1] // 2
    turned = jnp.concatenate([-values[..., half_width:], values[..., :half_width]], axis=-1)
    return values * cos_table + turned * sine_table

def project_rows(values, matrix):
    return jnp.einsum('bsd,df->bsf', values, matrix, precision=highest)

def block_forward(inputs, params):
    w_query, keyvalue_weight, w_out, w_gateup, w_down, norm_gains, head_gains = params
    batch_count, sequence_length, model_width = inputs.shape
    cos_table, sine_table = rope_tables(sequence_length, HEAD_DIM)
    cos_table = cos_table[:, None, :]
    sine_table = sine_table[:, None, :]
    normed_rows = lowered_gradient(lowered_input(rms_apply(inputs, norm_gains[0])))
    query_raw = lowered_gradient(project_rows(normed_rows, w_query)).reshape(batch_count, sequence_length, QUERY_COUNT, HEAD_DIM)
    key_unrotated = lowered_gradient(project_rows(normed_rows, keyvalue_weight[0])).reshape(batch_count, sequence_length, KEYVALUE_HEADS, HEAD_DIM)
    value_split = lowered_gradient(lowered_input(project_rows(normed_rows, keyvalue_weight[1]))).reshape(batch_count, sequence_length, KEYVALUE_HEADS, HEAD_DIM)
    query_split = lowered_input(rotate_pairs(rms_apply(query_raw, head_gains[0]), cos_table, sine_table))
    key_heads = lowered_input(rotate_pairs(rms_apply(key_unrotated, head_gains[1]), cos_table, sine_table))
    grouped_heads = query_split.reshape(batch_count, sequence_length, KEYVALUE_HEADS, QUERY_COUNT // KEYVALUE_HEADS, HEAD_DIM)
    scores = jnp.einsum('bqkgd,btkd->bkgqt', grouped_heads, key_heads, precision=highest) * HEAD_DIM ** (-0.5)
    causal = jnp.arange(sequence_length)[:, None] >= jnp.arange(sequence_length)[None, :]
    scores = lowered_gradient(jnp.where(causal, scores, -jnp.inf))
    row_top = lax.optimization_barrier(jnp.max(scores, axis=-1, keepdims=True))
    exponent = jnp.exp(scores - row_top)
    soft_weights = exponent / lax.optimization_barrier(jnp.sum(exponent, axis=-1, keepdims=True))
    attended = jnp.einsum('bkgqt,btkd->bqkgd', lowered_input(soft_weights), value_split, precision=highest)
    attended = lowered_gradient(lowered_input(attended.reshape(batch_count, sequence_length, QUERY_COUNT * HEAD_DIM)))
    middle = inputs + lowered_gradient(project_rows(attended, w_out))
    normed_two = lowered_gradient(lowered_input(rms_apply(middle, norm_gains[1])))
    gate_pre = lowered_gradient(project_rows(normed_two, w_gateup[0]))
    up_pre = lowered_gradient(project_rows(normed_two, w_gateup[1]))
    hidden = lowered_input(jax.nn.silu(gate_pre) * up_pre)
    return middle + lowered_gradient(project_rows(hidden, w_down))

def reference(section_input, cotangent, w_query, keyvalue_weight, w_out, w_gateup, w_down, norm_gains, head_gains):
    params = tuple((item.astype(jnp.float32) for item in (w_query, keyvalue_weight, w_out, w_gateup, w_down, norm_gains, head_gains)))
    group_count = SEQS // MICRO
    inputs = section_input.astype(jnp.float32).reshape(group_count, MICRO, SEQ, MODEL_DIM)
    cot_all = cotangent.astype(jnp.float32).reshape(group_count, MICRO, SEQ, MODEL_DIM)
    section_zero = tuple((item[0] for item in params))
    section_one = tuple((item[1] for item in params))

    def group_step(totals, batch_pair):
        first_in, cot_in = batch_pair
        out_zero, back_zero = jax.vjp(block_forward, first_in, section_zero)
        second_in = lowered_input(out_zero)
        out_one, back_one = jax.vjp(block_forward, second_in, section_one)
        grad_second, grads_one = back_one(cot_in)
        grad_second = lowered_input(grad_second)
        grad_first, grads_zero = back_zero(grad_second)
        totals = jax.tree.map(lambda acc_item, add_zero, add_one: acc_item + jnp.stack([add_zero, add_one]), totals, grads_zero, grads_one)
        return (totals, (second_in, out_one, grad_first, grad_second))
    zero_totals = tuple((jnp.zeros(item.shape, jnp.float32) for item in params))
    totals, emitted = lax.scan(group_step, zero_totals, (inputs, cot_all))
    sent_all, out_all, grad_first_all, grad_second_all = emitted
    section_out = jnp.stack([sent_all, out_all]).reshape(2, SEQS, SEQ, MODEL_DIM).astype(jnp.bfloat16)
    input_grads = jnp.stack([grad_first_all, grad_second_all]).reshape(2, SEQS, SEQ, MODEL_DIM).astype(jnp.bfloat16)
    return (section_out, input_grads, totals[0], totals[1], totals[2], totals[3], totals[4], totals[5], totals[6])
```

```python
import functools
import math

import jax
import jax.numpy as jnp
import numpy as np
from jax import lax
from jax.experimental import pallas as pl
from jax.experimental.pallas import tpu as pltpu
from jax.sharding import PartitionSpec as P

EPS = 1e-06
THETA = 1000000.0
MESH = pl.DeviceIdType.MESH
F32 = jnp.float32
BF16 = jnp.bfloat16

N1, OUT, N2, DOWN, DM, DN2, DA, DN1 = range(8)
WQ, WK, WV, WO, WG, WU, WD = range(7)


def mm(a, b):
    return jnp.dot(a, b, preferred_element_type=F32)


def mm_nt(a, b):
    return lax.dot_general(a, b, (((1,), (1,)), ((), ())), preferred_element_type=F32)


def mm_tn(a, b):
    return lax.dot_general(a, b, (((0,), (0,)), ((), ())), preferred_element_type=F32)


def inv_rms(v):
    return lax.rsqrt(jnp.mean(v * v, axis=-1, keepdims=True) + EPS)


def norm_back(dn, v, inv, gain):
    normal = v * inv
    inner = dn * gain
    dv = inv * (inner - normal * jnp.mean(inner * normal, axis=-1, keepdims=True))
    return dv, dn * normal


def tile_of(width, most):
    best = width
    for cand in range(128, min(width, most) + 1, 128):
        if width % cand == 0:
            best = cand
    return best


def kernel(
    cfg,
    x_in,
    c_in,
    wq_h,
    wkv_h,
    wo_h,
    wgu_h,
    wd_h,
    gn_in,
    cos_ref,
    sin_ref,
    y_ref,
    dx_ref,
    gq_o,
    gkv_o,
    go_o,
    ggu_o,
    gd_o,
    gain_o,
    wq,
    wk,
    wv,
    wo,
    wg,
    wu,
    wd,
    n1,
    n2,
    dm,
    da,
    qraw,
    kraw,
    qh,
    kh,
    vh,
    att,
    probs,
    gate,
    up,
    hid,
    mid,
    dmid,
    rs_send,
    rs_recv,
    datt,
    dq,
    dk,
    dv,
    gbuf,
    gains,
    gacc,
    gz,
    gdp,
    xb,
    dyb,
    z_send,
    z_recv,
    w_send,
    w_recv,
    g_send,
    g_recv,
    h_send,
    h_recv,
    s_send,
    s_recv,
    go_sem,
):
    n, an, bn, nt, micro, rows, width, head = cfg
    seq = rows * nt
    qw = wq.shape[1]
    kw = wk.shape[1]
    fw = wg.shape[1]
    q_heads = qw // head
    kv_heads = kw // head
    group = q_heads // kv_heads
    part = width // n
    scale = head ** (-0.5)

    p = lax.axis_index("pipe")
    t = lax.axis_index("tensor")
    d = lax.axis_index("dp")
    minor = lax.rem(d, an)
    major = d // an

    def rank(a, b):
        return lax.rem(major + b + bn, bn) * an + lax.rem(minor + a + an, an)

    barrier = pltpu.get_barrier_semaphore()
    for k in range(1, nt):
        pl.semaphore_signal(
            barrier, inc=1, device_id={"tensor": lax.rem(t + k, nt)}, device_id_type=MESH
        )
    for k in range(1, n):
        pl.semaphore_signal(
            barrier, inc=1, device_id={"dp": lax.rem(d + k, n)}, device_id_type=MESH
        )
    pl.semaphore_signal(barrier, inc=1, device_id={"pipe": 1 - p}, device_id_type=MESH)
    pl.semaphore_wait(barrier, nt - 1 + n - 1 + 1)

    sources = (
        wq_h,
        wkv_h.at[0],
        wkv_h.at[1],
        wo_h,
        wgu_h.at[0],
        wgu_h.at[1],
        wd_h,
    )
    fulls = (wq, wk, wv, wo, wg, wu, wd)
    by_columns = (False, False, False, True, False, False, True)

    def shard_half(k, h):
        half = sources[k].shape[0] // 2
        return sources[k].at[pl.ds(h * half, half), :]

    def full_half(k, block, h):
        half = sources[k].shape[0] // 2
        if by_columns[k]:
            return fulls[k].at[
                pl.ds(h * half, half), pl.ds(pl.multiple_of(block * part, part), part)
            ]
        return fulls[k].at[pl.ds(pl.multiple_of(block * part + h * half, half), half), :]

    def local_copy(k, h):
        return pltpu.make_async_copy(shard_half(k, h), full_half(k, d, h), w_send.at[k, h, 0])

    def own_copy(k, h, a, b):
        return pltpu.make_async_remote_copy(
            src_ref=shard_half(k, h),
            dst_ref=full_half(k, d, h),
            send_sem=w_send.at[k, h, a + b * an],
            recv_sem=w_recv.at[k, h, a + b * an],
            device_id={"dp": rank(a, b)},
            device_id_type=MESH,
        )

    def relay_copy(k, h, a, b):
        block = rank(-a, 0) if h == 0 else rank(0, -b)
        target = rank(0, b) if h == 0 else rank(a, 0)
        return pltpu.make_async_remote_copy(
            src_ref=full_half(k, block, h),
            dst_ref=full_half(k, block, h),
            send_sem=w_send.at[k, h, a + b * an],
            recv_sem=w_recv.at[k, h, a + b * an],
            device_id={"dp": target},
            device_id_type=MESH,
        )

    def arrival(k, h, a, b):
        block = rank(-a, -b)
        return pltpu.make_async_remote_copy(
            src_ref=full_half(k, block, h),
            dst_ref=full_half(k, block, h),
            send_sem=w_send.at[k, h, a + b * an],
            recv_sem=w_recv.at[k, h, a + b * an],
            device_id={"dp": rank(-a, -b)},
            device_id_type=MESH,
        )

    def own(*pieces):
        for k in pieces:
            for h in range(2):
                local_copy(k, h).start()
                for a in range(1, an):
                    own_copy(k, h, a, 0).start()
                for b in range(1, bn):
                    own_copy(k, h, 0, b).start()

    def relay(*pieces):
        for k in pieces:
            for a in range(1, an):
                arrival(k, 0, a, 0).wait_recv()
                for b in range(1, bn):
                    relay_copy(k, 0, a, b).start()
            for b in range(1, bn):
                arrival(k, 1, 0, b).wait_recv()
                for a in range(1, an):
                    relay_copy(k, 1, a, b).start()

    def arrive(*pieces):
        for k in pieces:
            for h in range(2):
                local_copy(k, h).wait()
            for b in range(1, bn):
                for a in range(an):
                    arrival(k, 0, a, b).wait_recv()
            for a in range(1, an):
                for b in range(bn):
                    arrival(k, 1, a, b).wait_recv()

    def gather_sent(*pieces):
        for k in pieces:
            for h in range(2):
                for a in range(1, an):
                    own_copy(k, h, a, 0).wait_send()
                for b in range(1, bn):
                    own_copy(k, h, 0, b).wait_send()
                for a in range(1, an):
                    for b in range(1, bn):
                        relay_copy(k, h, a, b).wait_send()

    landing = (gq_o, gkv_o, gkv_o, go_o, ggu_o, ggu_o, gd_o)

    def landing_block(k, slot):
        if k in (WK, WG):
            return landing[k].at[slot, 0]
        if k in (WV, WU):
            return landing[k].at[slot, 1]
        return landing[k].at[slot]

    def full_block(k, block):
        start = pl.multiple_of(block * part, part)
        if by_columns[k]:
            return fulls[k].at[:, pl.ds(start, part)]
        return fulls[k].at[pl.ds(start, part), :]

    def grad_local(k):
        return pltpu.make_async_copy(full_block(k, d), landing_block(k, 0), g_send.at[k, 0])

    def grad_copy(k, step):
        owner = lax.rem(d + step, n)
        return pltpu.make_async_remote_copy(
            src_ref=full_block(k, owner),
            dst_ref=landing_block(k, step),
            send_sem=g_send.at[k, step],
            recv_sem=g_recv.at[k, step],
            device_id={"dp": owner},
            device_id_type=MESH,
        )

    def grads_go(*pieces):
        for k in pieces:
            for step in range(1, n):
                grad_copy(k, step).start()
            grad_local(k).start()

    def grads_wait(*pieces):
        for k in pieces:
            grad_local(k).wait()
            for step in range(1, n):
                grad_copy(k, step).wait()

    def z_peer(k):
        return lax.rem(t + k, nt)

    def own_rows(m):
        return pl.ds(pl.multiple_of(m * seq + t * rows, rows), rows)

    def share_copy(stage, ref, m, k):
        return pltpu.make_async_remote_copy(
            src_ref=ref.at[own_rows(m), :],
            dst_ref=ref.at[own_rows(m), :],
            send_sem=z_send.at[stage, m, k - 1],
            recv_sem=z_recv.at[stage, m, k - 1],
            device_id={"tensor": z_peer(k)},
            device_id_type=MESH,
        )

    def share_start(stage, ref, m):
        for k in range(1, nt):
            share_copy(stage, ref, m, k).start()

    def share_wait(stage, ref, m):
        for k in range(1, nt):
            origin = lax.rem(t + nt - k, nt)
            spot = pl.ds(pl.multiple_of(m * seq + origin * rows, rows), rows)
            pltpu.make_async_remote_copy(
                src_ref=ref.at[spot, :],
                dst_ref=ref.at[spot, :],
                send_sem=z_send.at[stage, m, k - 1],
                recv_sem=z_recv.at[stage, m, k - 1],
                device_id={"tensor": origin},
                device_id_type=MESH,
            ).wait_recv()
        for k in range(1, nt):
            share_copy(stage, ref, m, k).wait_send()

    def spread_copy(stage, slot, m, k):
        peer = z_peer(k)
        return pltpu.make_async_remote_copy(
            src_ref=rs_send.at[pl.ds(pl.multiple_of(m * seq + peer * rows, rows), rows), :],
            dst_ref=rs_recv.at[slot, k - 1, pl.ds(pl.multiple_of(m * rows, rows), rows), :],
            send_sem=z_send.at[stage, m, k - 1],
            recv_sem=z_recv.at[stage, m, k - 1],
            device_id={"tensor": peer},
            device_id_type=MESH,
        )

    def spread_start(stage, slot, m):
        for k in range(1, nt):
            spread_copy(stage, slot, m, k).start()

    def spread_sum(stage, slot, m):
        for k in range(1, nt):
            spread_copy(stage, slot, m, k).wait()
        total = rs_send[own_rows(m), :].astype(F32)
        for k in range(1, nt):
            total += rs_recv[slot, k - 1, mine(m), :].astype(F32)
        return total

    def mine(m):
        return pl.ds(pl.multiple_of(m * rows, rows), rows)

    def tokens(m):
        return pl.ds(pl.multiple_of(m * seq, seq), seq)

    def columns(i, size):
        return pl.ds(pl.multiple_of(i * size, size), size)

    def hand_forward(m):
        return pltpu.make_async_remote_copy(
            src_ref=y_ref.at[mine(m), :],
            dst_ref=xb.at[mine(m), :],
            send_sem=h_send.at[0, m],
            recv_sem=h_recv.at[0, m],
            device_id={"pipe": 1 - p},
            device_id_type=MESH,
        )

    def hand_back(m):
        return pltpu.make_async_remote_copy(
            src_ref=dx_ref.at[mine(m), :],
            dst_ref=dyb.at[mine(m), :],
            send_sem=h_send.at[1, m],
            recv_sem=h_recv.at[1, m],
            device_id={"pipe": 1 - p},
            device_id_type=MESH,
        )

    def gain_copy(step):
        return pltpu.make_async_remote_copy(
            src_ref=gn_in,
            dst_ref=gbuf.at[step],
            send_sem=s_send.at[0, step],
            recv_sem=s_recv.at[0, step],
            device_id={"dp": lax.rem(d + step, n)},
            device_id_type=MESH,
        )

    def gain_z_copy(k):
        return pltpu.make_async_remote_copy(
            src_ref=gacc,
            dst_ref=gz.at[k],
            send_sem=s_send.at[1, k],
            recv_sem=s_recv.at[1, k],
            device_id={"tensor": z_peer(k)},
            device_id_type=MESH,
        )

    def gain_dp_copy(step):
        return pltpu.make_async_remote_copy(
            src_ref=gz.at[0],
            dst_ref=gdp.at[step],
            send_sem=s_send.at[2, step],
            recv_sem=s_recv.at[2, step],
            device_id={"dp": lax.rem(d + step, n)},
            device_id_type=MESH,
        )

    def dm_stage():
        @pl.loop(0, micro)
        def _(m):
            @pl.when(p == 0)
            def _():
                hand_back(m).wait_recv()

            dm[own_rows(m), :] = dyb[mine(m), :]
            share_start(DM, dm, m)

    for step in range(1, n):
        gain_copy(step).start()

    @pl.when(p == 1)
    def _():
        dyb[...] = c_in[...]
        pl.semaphore_wait(go_sem, 1)

    own(WQ, WK, WV, WO)

    @pl.when(p == 0)
    def _():
        xb[...] = x_in[...]

    gacc[...] = jnp.zeros_like(gacc)
    for step in range(1, n):
        gain_copy(step).wait()
    total_gain = gn_in[...]
    for step in range(1, n):
        total_gain += gbuf[step]
    gains[...] = total_gain

    @pl.when(p == 1)
    def _():
        dm_stage()
        own(WG)
        relay(WQ, WK, WV, WO)

    @pl.loop(0, micro)
    def _(m):
        @pl.when(p == 1)
        def _():
            hand_forward(m).wait_recv()

        v = xb[mine(m), :].astype(F32)
        n1[own_rows(m), :] = (v * inv_rms(v) * gains[0:1, :]).astype(BF16)
        share_start(N1, n1, m)

    @pl.when(p == 0)
    def _():
        own(WG)
        relay(WQ, WK, WV, WO)

    own(WU)
    arrive(WQ, WK, WV, WO)

    q_gain = gains[2:3, 0:head]
    k_gain = gains[3:4, 0:head]

    def rope(v):
        return v * cos_ref[...] + pltpu.roll(v, head // 2, 1) * sin_ref[...]

    def rope_back(g):
        return g * cos_ref[...] - pltpu.roll(g, head // 2, 1) * sin_ref[...]

    @pl.loop(0, micro)
    def _(m):
        share_wait(N1, n1, m)
        tok = tokens(m)
        tile = tile_of(qw, 256)

        @pl.loop(0, qw // tile)
        def _(i):
            qraw[tok, columns(i, tile)] = mm(n1[tok, :], wq[:, columns(i, tile)])

        kraw[tok, :] = mm(n1[tok, :], wk[...])
        vh[tok, :] = mm(n1[tok, :], wv[...]).astype(BF16)

        @pl.loop(0, q_heads)
        def _(h):
            v = qraw[tok, columns(h, head)]
            qh[tok, columns(h, head)] = rope(v * inv_rms(v) * q_gain).astype(BF16)

        @pl.loop(0, kv_heads)
        def _(h):
            v = kraw[tok, columns(h, head)]
            kh[tok, columns(h, head)] = rope(v * inv_rms(v) * k_gain).astype(BF16)

        causal = lax.broadcasted_iota(jnp.int32, (seq, seq), 0) >= lax.broadcasted_iota(
            jnp.int32, (seq, seq), 1
        )

        @pl.loop(0, q_heads)
        def _(h):
            scores = mm_nt(qh[tok, columns(h, head)], kh[tok, columns(h // group, head)]) * scale
            scores = jnp.where(causal, scores, -jnp.inf)
            top = jnp.max(scores, axis=-1, keepdims=True)
            ex = jnp.exp(scores - top)
            soft = (ex / jnp.sum(ex, axis=-1, keepdims=True)).astype(BF16)
            probs[pl.ds(pl.multiple_of((m * q_heads + h) * seq, seq), seq), :] = soft
            att[tok, columns(h, head)] = mm(soft, vh[tok, columns(h // group, head)]).astype(BF16)

        tile = tile_of(width, 512)

        @pl.loop(0, width // tile)
        def _(i):
            rs_send[tok, columns(i, tile)] = mm(att[tok, :], wo[:, columns(i, tile)]).astype(BF16)

        spread_start(OUT, 0, m)

    relay(WG)
    own(WD)

    @pl.loop(0, micro)
    def _(m):
        v = xb[mine(m), :].astype(F32) + spread_sum(OUT, 0, m)
        mid[mine(m), :] = v
        n2[own_rows(m), :] = (v * inv_rms(v) * gains[1:2, :]).astype(BF16)
        share_start(N2, n2, m)

    relay(WU)
    arrive(WG, WU)
    ff_tile = tile_of(fw, 256)

    @pl.loop(0, micro)
    def _(m):
        share_wait(N2, n2, m)
        tok = tokens(m)

        @pl.loop(0, fw // ff_tile)
        def _(i):
            cols = columns(i, ff_tile)
            g = mm(n2[tok, :], wg[:, cols])
            u = mm(n2[tok, :], wu[:, cols])
            gate[tok, cols] = g.astype(BF16)
            up[tok, cols] = u.astype(BF16)
            hid[tok, cols] = (g * jax.nn.sigmoid(g) * u).astype(BF16)

        @pl.when(m == 0)
        def _():
            relay(WD)

            @pl.when(p == 0)
            def _():
                pl.semaphore_signal(
                    go_sem, inc=1, device_id={"pipe": 1 - p}, device_id_type=MESH
                )

            arrive(WD)

        tile = tile_of(width, 256)

        @pl.loop(0, width // tile)
        def _(i):
            rs_send[tok, columns(i, tile)] = mm(hid[tok, :], wd[:, columns(i, tile)]).astype(BF16)

        spread_start(DOWN, 1, m)

    @pl.loop(0, micro)
    def _(m):
        y_ref[mine(m), :] = (mid[mine(m), :] + spread_sum(DOWN, 1, m)).astype(BF16)

        @pl.when(p == 0)
        def _():
            hand_forward(m).start()

    @pl.when(p == 0)
    def _():
        dm_stage()

    @pl.loop(0, micro)
    def _(m):
        share_wait(DM, dm, m)
        tok = tokens(m)

        @pl.loop(0, fw // ff_tile)
        def _(i):
            cols = columns(i, ff_tile)
            dh = mm_nt(dm[tok, :], wd[cols, :])
            g = gate[tok, cols].astype(F32)
            u = up[tok, cols].astype(F32)
            sig = jax.nn.sigmoid(g)
            gate[tok, cols] = (dh * u * sig * (1.0 + g * (1.0 - sig))).astype(BF16)
            up[tok, cols] = (dh * g * sig).astype(BF16)

        tile = tile_of(width, 256)

        @pl.loop(0, width // tile)
        def _(i):
            cols = columns(i, tile)
            rs_send[tok, cols] = (
                mm_nt(gate[tok, :], wg[cols, :]) + mm_nt(up[tok, :], wu[cols, :])
            ).astype(BF16)

        spread_start(DN2, 0, m)

    gather_sent(WQ, WK, WV, WO, WG, WU, WD)

    row_tile = tile_of(fw, 256)

    @pl.loop(0, fw // row_tile)
    def _(i):
        wd[columns(i, row_tile), :] = mm_tn(hid[:, columns(i, row_tile)], dm[...]).astype(BF16)

    grads_go(WD)
    wide_tile = tile_of(width, 256)

    @pl.loop(0, micro)
    def _(m):
        dn = spread_sum(DN2, 0, m).astype(BF16).astype(F32)
        v = mid[mine(m), :]
        dvec, terms = norm_back(dn, v, inv_rms(v), gains[1:2, :])
        gacc[1:2, :] += jnp.sum(terms, axis=0, keepdims=True)
        dvec += dyb[mine(m), :].astype(F32)
        dmid[mine(m), :] = dvec
        da[own_rows(m), :] = dvec.astype(BF16)
        share_start(DA, da, m)

    @pl.loop(0, width // wide_tile)
    def _(i):
        cols = columns(i, wide_tile)
        wg[cols, :] = mm_tn(n2[:, cols], gate[...]).astype(BF16)
        wu[cols, :] = mm_tn(n2[:, cols], up[...]).astype(BF16)

    grads_go(WG, WU)

    @pl.loop(0, micro)
    def _(m):
        share_wait(DA, da, m)
        tok = tokens(m)
        tile = tile_of(qw, 256)

        @pl.loop(0, qw // tile)
        def _(i):
            datt[:, columns(i, tile)] = mm_nt(da[tok, :], wo[columns(i, tile), :]).astype(BF16)

        @pl.loop(0, kv_heads)
        def _(c):
            kcols = columns(c, head)
            k_head = kh[tok, kcols]
            v_head = vh[tok, kcols]
            dv_sum = jnp.zeros((seq, head), F32)
            dk_sum = jnp.zeros((seq, head), F32)
            for j in range(group):
                h = c * group + j
                qcols = columns(h, head)
                dah = datt[:, qcols]
                soft = probs[pl.ds(pl.multiple_of((m * q_heads + h) * seq, seq), seq), :]
                dp = mm_nt(dah, v_head)
                dv_sum += mm_tn(soft, dah)
                soft = soft.astype(F32)
                ds = (soft * (dp - jnp.sum(soft * dp, axis=-1, keepdims=True))).astype(BF16)
                dqh = rope_back(mm(ds, k_head) * scale)
                dk_sum += mm_tn(ds, qh[tok, qcols])
                v = qraw[tok, qcols]
                grad, terms = norm_back(dqh, v, inv_rms(v), q_gain)
                dq[tok, qcols] = grad.astype(BF16)
                gacc[2:3, 0:head] += jnp.sum(terms, axis=0, keepdims=True)
            v = kraw[tok, kcols]
            grad, terms = norm_back(rope_back(dk_sum * scale), v, inv_rms(v), k_gain)
            dk[tok, kcols] = grad.astype(BF16)
            gacc[3:4, 0:head] += jnp.sum(terms, axis=0, keepdims=True)
            dv[tok, kcols] = dv_sum.astype(BF16)

        tile = tile_of(width, 512)

        @pl.loop(0, width // tile)
        def _(i):
            cols = columns(i, tile)
            rs_send[tok, cols] = (
                mm_nt(dq[tok, :], wq[cols, :])
                + mm_nt(dk[tok, :], wk[cols, :])
                + mm_nt(dv[tok, :], wv[cols, :])
            ).astype(BF16)

        spread_start(DN1, 1, m)

    @pl.loop(0, qw // tile_of(qw, 256))
    def _(i):
        cols = columns(i, tile_of(qw, 256))
        wo[cols, :] = mm_tn(att[:, cols], da[...]).astype(BF16)

    grads_go(WO)

    @pl.loop(0, micro)
    def _(m):
        dn = spread_sum(DN1, 1, m).astype(BF16).astype(F32)
        v = xb[mine(m), :].astype(F32)
        dvec, terms = norm_back(dn, v, inv_rms(v), gains[0:1, :])
        gacc[0:1, :] += jnp.sum(terms, axis=0, keepdims=True)
        dx_ref[mine(m), :] = (dmid[mine(m), :] + dvec).astype(BF16)

        @pl.when(p == 1)
        def _():
            hand_back(m).start()

    for k in range(1, nt):
        gain_z_copy(k).start()

    @pl.loop(0, width // wide_tile)
    def _(i):
        cols = columns(i, wide_tile)
        wq[cols, :] = mm_tn(n1[:, cols], dq[...]).astype(BF16)
        wk[cols, :] = mm_tn(n1[:, cols], dk[...]).astype(BF16)
        wv[cols, :] = mm_tn(n1[:, cols], dv[...]).astype(BF16)

    grads_go(WQ, WK, WV)

    for k in range(1, nt):
        gain_z_copy(k).wait()
    total_gain = gacc[...]
    for k in range(1, nt):
        total_gain += gz[k]
    gz[0] = total_gain
    for step in range(1, n):
        gain_dp_copy(step).start()
    for step in range(1, n):
        gain_dp_copy(step).wait()
    for step in range(1, n):
        total_gain += gdp[step]
    gain_o[...] = total_gain

    @pl.loop(0, micro)
    def _(m):
        @pl.when(p == 0)
        def _():
            hand_forward(m).wait_send()

        @pl.when(p == 1)
        def _():
            hand_back(m).wait_send()

    grads_wait(WD, WG, WU, WO, WQ, WK, WV)


def rope_tables(seq, head):
    half = head // 2
    frequency = THETA ** (-2.0 * np.arange(half, dtype=np.float64) / head)
    angles = np.arange(seq, dtype=np.float64)[:, None] * frequency[None, :]
    angles = np.concatenate([angles, angles], axis=-1)
    sign = np.where(np.arange(head) < half, -1.0, 1.0)[None, :]
    return np.cos(angles).astype(np.float32), (np.sin(angles) * sign).astype(np.float32)


def per_device(
    n, nt, section_input, cotangent, w_query, keyvalue, w_out, w_gateup, w_down, norm_gains, head_gains
):
    micro, rows, width = section_input.shape
    part = norm_gains.shape[2]
    head_part = head_gains.shape[2]
    head = head_part * n
    seq = rows * nt
    tok = micro * seq
    qw = w_query.shape[2]
    kw = keyvalue.shape[3]
    fw = w_gateup.shape[3]
    an = 1
    for cand in range(1, math.isqrt(n) + 1):
        if n % cand == 0:
            an = cand
    bn = n // an
    d = lax.axis_index("dp")

    placed = jnp.zeros((8, width), F32)
    placed = lax.dynamic_update_slice(placed, norm_gains[0].astype(F32), (0, d * part))
    placed = lax.dynamic_update_slice(placed, head_gains[0].astype(F32), (2, d * head_part))
    cos, sin = rope_tables(seq, head)

    def vm(*shape, dtype=BF16):
        return pltpu.VMEM(shape, dtype)

    q_heads = qw // head
    scratch = [
        vm(width, qw),
        vm(width, kw),
        vm(width, kw),
        vm(qw, width),
        vm(width, fw),
        vm(width, fw),
        vm(fw, width),
        vm(tok, width),
        vm(tok, width),
        vm(tok, width),
        vm(tok, width),
        vm(tok, qw, dtype=F32),
        vm(tok, kw, dtype=F32),
        vm(tok, qw),
        vm(tok, kw),
        vm(tok, kw),
        vm(tok, qw),
        vm(micro * q_heads * seq, seq),
        vm(tok, fw),
        vm(tok, fw),
        vm(tok, fw),
        vm(micro * rows, width, dtype=F32),
        vm(micro * rows, width, dtype=F32),
        vm(tok, width),
        vm(2, nt - 1, micro * rows, width),
        vm(seq, qw),
        vm(tok, qw),
        vm(tok, kw),
        vm(tok, kw),
        vm(n, 8, width, dtype=F32),
        vm(8, width, dtype=F32),
        vm(8, width, dtype=F32),
        vm(nt, 8, width, dtype=F32),
        vm(n, 8, width, dtype=F32),
        vm(micro * rows, width),
        vm(micro * rows, width),
        pltpu.SemaphoreType.DMA((8, micro, nt - 1)),
        pltpu.SemaphoreType.DMA((8, micro, nt - 1)),
        pltpu.SemaphoreType.DMA((7, 2, n)),
        pltpu.SemaphoreType.DMA((7, 2, n)),
        pltpu.SemaphoreType.DMA((7, n)),
        pltpu.SemaphoreType.DMA((7, n)),
        pltpu.SemaphoreType.DMA((2, micro)),
        pltpu.SemaphoreType.DMA((2, micro)),
        pltpu.SemaphoreType.DMA((3, max(n, nt))),
        pltpu.SemaphoreType.DMA((3, max(n, nt))),
        pltpu.SemaphoreType.REGULAR,
    ]
    vmem = pl.BlockSpec(memory_space=pltpu.VMEM)
    hbm = pl.BlockSpec(memory_space=pl.ANY)
    shape = jax.ShapeDtypeStruct
    y, dx, gq, gkv, go, ggu, gd, gain = pl.pallas_call(
        functools.partial(kernel, (n, an, bn, nt, micro, rows, width, head)),
        out_shape=(
            shape((micro * rows, width), BF16),
            shape((micro * rows, width), BF16),
            shape((n, part, qw), BF16),
            shape((n, 2, part, kw), BF16),
            shape((n, qw, part), BF16),
            shape((n, 2, part, fw), BF16),
            shape((n, fw, part), BF16),
            shape((8, width), F32),
        ),
        in_specs=[vmem, vmem, hbm, hbm, hbm, hbm, hbm, vmem, vmem, vmem],
        out_specs=(vmem, vmem, hbm, hbm, hbm, hbm, hbm, vmem),
        scratch_shapes=scratch,
        compiler_params=pltpu.CompilerParams(
            collective_id=0, has_side_effects=True, vmem_limit_bytes=60 * 2**20
        ),
    )(
        section_input.reshape(micro * rows, width),
        cotangent.reshape(micro * rows, width),
        w_query[0],
        keyvalue[0],
        w_out[0],
        w_gateup[0],
        w_down[0],
        placed,
        jnp.asarray(cos),
        jnp.asarray(sin),
    )

    def total(blocks):
        return jnp.sum(blocks.astype(F32), axis=0)[None]

    return (
        y.reshape(1, micro, rows, width),
        dx.reshape(1, micro, rows, width),
        total(gq),
        total(gkv),
        total(go),
        total(ggu),
        total(gd),
        lax.dynamic_slice(gain, (0, d * part), (2, part))[None],
        lax.dynamic_slice(gain, (2, d * head_part), (2, head_part))[None],
    )


def solution(mesh):
    in_specs = (
        P("dp", "tensor", None),
        P("dp", "tensor", None),
        P("pipe", "dp", "tensor"),
        P("pipe", None, "dp", "tensor"),
        P("pipe", "tensor", "dp"),
        P("pipe", None, "dp", "tensor"),
        P("pipe", "tensor", "dp"),
        P("pipe", None, "dp"),
        P("pipe", None, "dp"),
    )
    out_specs = (
        P("pipe", "dp", "tensor", None),
        P("pipe", "dp", "tensor", None),
        P("pipe", "dp", "tensor"),
        P("pipe", None, "dp", "tensor"),
        P("pipe", "tensor", "dp"),
        P("pipe", None, "dp", "tensor"),
        P("pipe", "tensor", "dp"),
        P("pipe", None, "dp"),
        P("pipe", None, "dp"),
    )
    return jax.shard_map(
        functools.partial(per_device, mesh.shape["dp"], mesh.shape["tensor"]),
        mesh=mesh,
        in_specs=in_specs,
        out_specs=out_specs,
        check_vma=False,
    )
```
